32 devices in a mesh: row: 4 (over x, core), col: 8 (over z, y).
Axes of the slice: x: 2, y: 2, z: 4, core: 2. Of those that a mesh axis runs over, the one named last changes fastest.
Arguments:
- scalar_field: bfloat16 [768, 768, 1024], P('row', 'col'), may hold values from -6 to 6
- x_operator: bfloat16 [1024, 1024], replicated, may hold values from -0.1875 to 0.1875
- y_second: bfloat16 [768, 768], replicated, may hold values from -0.21875 to 0.21875
- y_first: bfloat16 [768, 768], replicated, may hold values from -0.21875 to 0.21875
- y_stretch: float32 [768], replicated, may hold values from 0.5 to 2
- y_curve: float32 [768], replicated, may hold values from -3 to 3
- z_operator: bfloat16 [768, 768], replicated, may hold values from -0.21875 to 0.21875
Outputs:
- diffusion: bfloat16 [768, 768, 1024], P('row', 'col')
The draws below stay inside these ranges and needn't reach their ends.
All inputs are finite; a program needn't handle non-finite values.
Results may differ from the reference program's by a relative error of at most 0.0052.
Values may be sent and summed in bfloat16 or wider, within the bound.
No kernel may reach another device: no remote copies, remote signals or barrier semaphores. Data moves between devices by JAX's collectives and lax.ppermute only.
A program may use at most 384 MiB of HBM per device.

```python
import math
import jax
import jax.numpy as jnp
from jax import lax

NX = 1024
NY = 768
NZ = 768
N_COL = 8


def levels(key, shape, pieces, least, largest):
    loudness, own = 1.0, jax.random.fold_in(key, 6)
    for position, blocks in pieces:
        draws = jnp.exp(jax.random.uniform(jax.random.fold_in(own, position), (blocks,), jnp.float32, least / len(pieces), largest / len(pieces)))
        loudness = loudness * jnp.repeat(draws, shape[position] // blocks).reshape([-1 if axis == position else 1 for axis in range(len(shape))])
    return loudness


def scatter_about(own_key, dims, deviation, bound, pieces=(), held_as=jnp.bfloat16):
    loudness = levels(own_key, dims, pieces, -0.22, 0.18) if pieces else 1.0
    values = jax.random.normal(own_key, dims, jnp.float32) * deviation * loudness
    return jnp.minimum(jnp.maximum(values, -bound), bound).astype(held_as)


def setup_inputs(seed: int = 0) -> dict:
    key_of = jax.random.split(jax.random.key(seed), 8)
    scalar_field = scatter_about(key_of[0], (NY, NZ, NX), 1.0, 6.0, ((0, 4), (1, 8)))
    x_operator = scatter_about(key_of[1], (NX, NX), NX ** -0.5, 0.1875)
    y_second = scatter_about(key_of[2], (NY, NY), NY ** -0.5, 0.21875)
    y_first = scatter_about(key_of[3], (NY, NY), NY ** -0.5, 0.21875)
    y_stretch = jnp.clip(jnp.exp(jax.random.uniform(key_of[4], (NY,), jnp.float32, math.log(0.5), math.log(2.0))), 0.5, 2.0)
    y_curve = scatter_about(key_of[5], (NY,), 0.6, 3.0, (), jnp.float32)
    z_operator = scatter_about(key_of[6], (NZ, NZ), NZ ** -0.5, 0.21875)
    return {"scalar_field": scalar_field, "x_operator": x_operator, "y_second": y_second, "y_first": y_first, "y_stretch": y_stretch, "y_curve": y_curve, "z_operator": z_operator}


def reference(scalar_field, x_operator, y_second, y_first, y_stretch, y_curve, z_operator):
    y_combined = (y_stretch[None, :] * y_second.astype(jnp.float32) + y_curve[None, :] * y_first.astype(jnp.float32)).astype(jnp.bfloat16)
    z_blocks = N_COL
    y_size = NY // z_blocks

    def z_apply(planes_in):
        z_full = jnp.einsum('yzx,zk->ykx', planes_in.astype(jnp.float32), z_operator.astype(jnp.float32))
        return z_full.astype(jnp.bfloat16)

    by_rows = scalar_field.reshape(z_blocks, y_size, NZ, NX)
    z_term = lax.map(z_apply, by_rows).reshape(NY, NZ, NX)

    z_size = NZ // z_blocks
    field_cols = jnp.moveaxis(scalar_field.reshape(NY, z_blocks, z_size, NX), 1, 0)
    zterm_cols = jnp.moveaxis(z_term.reshape(NY, z_blocks, z_size, NX), 1, 0)

    def combine(inputs):
        column_in, z_part = inputs
        x_term = jnp.einsum('yzx,xk->yzk', column_in.astype(jnp.float32), x_operator.astype(jnp.float32))
        y_term = jnp.einsum('yzx,yk->kzx', column_in.astype(jnp.float32), y_combined.astype(jnp.float32)).astype(jnp.bfloat16)
        total = x_term + y_term.astype(jnp.float32) + z_part.astype(jnp.float32)
        return total.astype(jnp.bfloat16)

    result = lax.map(combine, (field_cols, zterm_cols))
    return jnp.moveaxis(result, 0, 1).reshape(NY, NZ, NX)
```

```python
import functools
import math

import jax
import jax.numpy as jnp
from jax import lax
from jax.experimental import pallas as pl
from jax.experimental.pallas import tpu as pltpu
from jax.sharding import PartitionSpec as P

VMEM_BYTES = 56 * 1024 * 1024


def z_kernel(operator_ref, field_ref, out_ref):
    parts, rows, depth, width = field_ref.shape
    for row in range(rows):
        planes = field_ref[:, row]
        if depth % 16:
            planes = planes.astype(jnp.float32)
        planes = planes.reshape(parts * depth, width).astype(jnp.bfloat16)
        product = jnp.dot(operator_ref[...], planes, preferred_element_type=jnp.float32)
        out_ref[:, row] = product.reshape(parts, depth, width).astype(jnp.bfloat16)


def z_apply(operator, field, first, count, step):
    parts, rows, depth, width = field.shape
    offset = first // step
    points = parts * depth
    return pl.pallas_call(
        z_kernel,
        grid=(count // step,),
        in_specs=[
            pl.BlockSpec((points, points), lambda i: (0, 0)),
            pl.BlockSpec((parts, step, depth, width), lambda i: (0, i + offset, 0, 0)),
        ],
        out_specs=pl.BlockSpec((parts, step, depth, width), lambda i: (0, i, 0, 0)),
        out_shape=jax.ShapeDtypeStruct((parts, count, depth, width), jnp.bfloat16),
        compiler_params=pltpu.CompilerParams(vmem_limit_bytes=VMEM_BYTES),
        cost_estimate=pl.CostEstimate(
            flops=2 * points * points * count * width,
            bytes_accessed=4 * points * count * width,
            transcendentals=0,
        ),
    )(operator, field)


def total_kernel(slabs, row_ref, operator_ref, field_ref, z_ref, *refs):
    y_refs, out_ref, total = refs[: 2 * slabs], refs[-2], refs[-1]
    parts, rows, depth, width = total.shape
    flat = field_ref[...]
    if depth % 16:
        flat = flat.astype(jnp.float32)
    flat = flat.reshape(parts * rows * depth, width).astype(jnp.bfloat16)
    product = jnp.dot(flat, operator_ref[...], preferred_element_type=jnp.float32)
    total[...] = product.reshape(parts, rows, depth, width) + z_ref[...].astype(jnp.float32)
    share = width // slabs // 2
    for half in range(2):
        for distance in range(slabs):
            first = (2 * (row_ref[0] ^ distance) + half) * share
            lanes = pl.ds(pl.multiple_of(first, share), share)
            total[:, :, :, lanes] += y_refs[half * slabs + distance][...].astype(jnp.float32)
    out_ref[...] = total[...].astype(jnp.bfloat16)


def total_into(so_far, first, step, together, row, operator, field, z_term, y_terms):
    parts, count, depth, width = z_term.shape
    offset = first // step
    share = y_terms[0].shape[3]
    here = pl.BlockSpec((together, step, depth, width), lambda p, i, r: (p, i + offset, 0, 0))
    in_specs = [
        pl.BlockSpec((width, width), lambda p, i, r: (0, 0)),
        here,
        pl.BlockSpec((together, step, depth, width), lambda p, i, r: (p, i, 0, 0)),
    ] + [
        pl.BlockSpec((together, step, depth, share), lambda p, i, r: (p, i + offset, 0, 0))
        for _ in y_terms
    ]
    operands = [operator, field, z_term, *y_terms]
    aliases = {}
    if so_far is not None:
        in_specs.append(pl.BlockSpec(memory_space=pl.ANY))
        operands.append(so_far)
        aliases = {len(operands): 0}
    return pl.pallas_call(
        functools.partial(total_kernel, len(y_terms) // 2),
        grid_spec=pltpu.PrefetchScalarGridSpec(
            num_scalar_prefetch=1,
            grid=(parts // together, count // step),
            in_specs=in_specs,
            out_specs=here,
            scratch_shapes=[pltpu.VMEM((together, step, depth, width), jnp.float32)],
        ),
        out_shape=jax.ShapeDtypeStruct(field.shape, jnp.bfloat16),
        input_output_aliases=aliases,
        compiler_params=pltpu.CompilerParams(vmem_limit_bytes=VMEM_BYTES),
        cost_estimate=pl.CostEstimate(
            flops=2 * width * width * parts * count * depth,
            bytes_accessed=8 * width * parts * count * depth,
            transcendentals=0,
        ),
    )(row, *operands)


def swap(value, axis, size, distance):
    return lax.ppermute(value, axis, [(i, i ^ distance) for i in range(size)])


def chunk_sizes(share):
    end = max(1, share // 12)
    middle = share - 2 * end
    if middle < 2 * end:
        return [share]
    second = (2 * middle // 5) // end * end
    return [end, middle - second, second, end]


def per_device(rows, cols, scalar_field, x_operator, y_second, y_first, y_stretch, y_curve, z_operator):
    ny, nz, nx = scalar_field.shape
    me = lax.axis_index("row")
    y_combined = (
        y_stretch[None, :] * y_second.astype(jnp.float32)
        + y_curve[None, :] * y_first.astype(jnp.float32)
    ).astype(jnp.bfloat16)
    z_transposed = z_operator.T

    share = ny // cols
    planes = lax.all_to_all(scalar_field, "col", 0, 0, tiled=True)

    half = nx // rows // 2
    y_blocks = y_combined.reshape(rows, ny, rows, ny)
    by_distance = jnp.stack([y_blocks[me ^ d] for d in range(rows)])
    by_distance = jnp.stack([by_distance[:, :, me ^ d] for d in range(rows)], axis=2)
    by_distance = by_distance.reshape(rows * ny, rows, ny)

    def y_pencil(side):
        pieces = []
        for d in range(rows):
            first = (2 * (me ^ d) + side) * half
            piece = lax.dynamic_slice_in_dim(scalar_field, first, half, 2)
            pieces.append(piece if d == 0 else swap(piece, "row", rows, d))
        return jnp.concatenate(pieces, axis=0)

    def y_multiply(pencil):
        product = jnp.einsum(
            "yzx,ydk->dkzx", pencil, by_distance, preferred_element_type=jnp.float32
        ).astype(jnp.bfloat16)
        return [product[d] for d in range(rows)]

    def y_return(pieces):
        back = [pieces[d] if d == 0 else swap(pieces[d], "row", rows, d) for d in range(rows)]
        return [value.reshape(cols, share, nz, half) for value in back]

    pencils = [y_pencil(side) for side in range(2)]
    y_first_half, y_second_half = [y_multiply(pencil) for pencil in pencils]
    y_first_half = y_return(y_first_half)
    planes, y_first_half, y_second_half = lax.optimization_barrier(
        (planes, y_first_half, y_second_half)
    )
    y_second_half = y_return(y_second_half)

    planes = planes.reshape(cols, share, nz, nx)
    field = scalar_field.reshape(cols, share, nz, nx)
    where = me.reshape(1).astype(jnp.int32)
    sizes = chunk_sizes(share)
    step = math.gcd(*sizes)
    starts = [sum(sizes[:c]) for c in range(len(sizes))]
    last = len(sizes) - 1

    def z_chunk(c):
        return z_apply(z_transposed, planes, starts[c], sizes[c], step)

    def z_return(product):
        flat = product.reshape(-1, nz, nx)
        return lax.all_to_all(flat, "col", 0, 0, tiled=True).reshape(product.shape)

    def add_chunk(result, c, z_term):
        together = math.gcd(cols, 2 if c == last else 4)
        y_terms = y_first_half + y_second_half
        return total_into(
            result, starts[c], step, together, where, x_operator, field, z_term, y_terms
        )

    z_back, result = [], None
    for c in range(len(sizes)):
        product = z_chunk(c)
        if c == max(last - 1, 0):
            product, y_second_half = lax.optimization_barrier((product, y_second_half))
        if c == last and last >= 2:
            for earlier in range(last - 1):
                result = add_chunk(result, earlier, z_back[earlier])
            product, result = lax.optimization_barrier((product, result))
        z_back.append(z_return(product))
    for c in range(max(last - 1, 0), len(sizes)):
        result = add_chunk(result, c, z_back[c])
    return result.reshape(ny, nz, nx)


def solution(mesh):
    rows, cols = mesh.shape["row"], mesh.shape["col"]
    in_specs = (P("row", "col", None), P(), P(), P(), P(), P(), P())
    return jax.shard_map(
        functools.partial(per_device, rows, cols),
        mesh=mesh,
        in_specs=in_specs,
        out_specs=P("row", "col", None),
        check_vma=False,
    )
```

```python
import functools
import math

import jax
import jax.numpy as jnp
from jax import lax
from jax.experimental import pallas as pl
from jax.experimental.pallas import tpu as pltpu
from jax.sharding import PartitionSpec as P

VMEM_BYTES = 56 * 1024 * 1024


def z_kernel(operator_ref, field_ref, out_ref):
    parts, rows, depth, width = field_ref.shape
    for row in range(rows):
        planes = field_ref[:, row]
        if depth % 16:
            planes = planes.astype(jnp.float32)
        planes = planes.reshape(parts * depth, width).astype(jnp.bfloat16)
        product = jnp.dot(operator_ref[...], planes, preferred_element_type=jnp.float32)
        out_ref[:, row] = product.reshape(parts, depth, width).astype(jnp.bfloat16)


def z_apply(operator, field, first, count):
    parts, rows, depth, width = field.shape
    points = parts * depth
    return pl.pallas_call(
        z_kernel,
        grid=(count,),
        in_specs=[
            pl.BlockSpec((points, points), lambda i: (0, 0)),
            pl.BlockSpec((parts, 1, depth, width), lambda i: (0, i + first, 0, 0)),
        ],
        out_specs=pl.BlockSpec((parts, 1, depth, width), lambda i: (0, i, 0, 0)),
        out_shape=jax.ShapeDtypeStruct((parts, count, depth, width), jnp.bfloat16),
        compiler_params=pltpu.CompilerParams(vmem_limit_bytes=VMEM_BYTES),
        cost_estimate=pl.CostEstimate(
            flops=2 * points * points * count * width,
            bytes_accessed=4 * points * count * width,
            transcendentals=0,
        ),
    )(operator, field)


def total_kernel(slabs, row_ref, operator_ref, field_ref, z_ref, *refs):
    y_refs, out_ref = refs[: 2 * slabs], refs[-1]
    parts, rows, depth, width = out_ref.shape
    slab = width // slabs
    share = slab // 2

    def add_all(me):
        flat = field_ref[...]
        if depth % 16:
            flat = flat.astype(jnp.float32)
        flat = flat.reshape(parts * rows * depth, width).astype(jnp.bfloat16)
        for owner in range(slabs):
            lanes = slice(owner * slab, (owner + 1) * slab)
            product = jnp.dot(flat, operator_ref[:, lanes], preferred_element_type=jnp.float32)
            product = product.reshape(parts, rows, depth, slab)
            for half in range(2):
                here = slice(owner * slab + half * share, owner * slab + (half + 1) * share)
                y_term = y_refs[half * slabs + (owner ^ me)][...].astype(jnp.float32)
                z_term = z_ref[:, :, :, here].astype(jnp.float32)
                x_term = product[:, :, :, half * share : (half + 1) * share]
                out_ref[:, :, :, here] = (x_term + y_term + z_term).astype(jnp.bfloat16)

    for me in range(slabs):
        pl.when(row_ref[0] == me)(functools.partial(add_all, me))


def total_into(so_far, first, together, row, operator, field, z_term, y_terms):
    parts, count, depth, width = z_term.shape
    share = y_terms[0].shape[3]
    here = pl.BlockSpec((together, 1, depth, width), lambda p, i, r: (p, i + first, 0, 0))
    in_specs = [
        pl.BlockSpec((width, width), lambda p, i, r: (0, 0)),
        here,
        pl.BlockSpec((together, 1, depth, width), lambda p, i, r: (p, i, 0, 0)),
    ] + [
        pl.BlockSpec((together, 1, depth, share), lambda p, i, r: (p, i + first, 0, 0))
        for _ in y_terms
    ]
    operands = [operator, field, z_term, *y_terms]
    aliases = {}
    if so_far is not None:
        in_specs.append(pl.BlockSpec(memory_space=pl.ANY))
        operands.append(so_far)
        aliases = {len(operands): 0}
    return pl.pallas_call(
        functools.partial(total_kernel, len(y_terms) // 2),
        grid_spec=pltpu.PrefetchScalarGridSpec(
            num_scalar_prefetch=1,
            grid=(parts // together, count),
            in_specs=in_specs,
            out_specs=here,
        ),
        out_shape=jax.ShapeDtypeStruct(field.shape, jnp.bfloat16),
        input_output_aliases=aliases,
        compiler_params=pltpu.CompilerParams(vmem_limit_bytes=VMEM_BYTES // 2),
        cost_estimate=pl.CostEstimate(
            flops=2 * width * width * parts * count * depth,
            bytes_accessed=8 * width * parts * count * depth,
            transcendentals=0,
        ),
    )(row, *operands)


def swap(value, axis, size, distance):
    return lax.ppermute(value, axis, [(i, i ^ distance) for i in range(size)])


def chunk_sizes(share):
    if share < 3:
        return [share]
    last = 2 if share >= 12 else 1
    return [1, share - 1 - last, last]


def per_device(rows, cols, scalar_field, x_operator, y_second, y_first, y_stretch, y_curve, z_operator):
    ny, nz, nx = scalar_field.shape
    me = lax.axis_index("row")
    y_combined = (
        y_stretch[None, :] * y_second.astype(jnp.float32)
        + y_curve[None, :] * y_first.astype(jnp.float32)
    ).astype(jnp.bfloat16)
    z_transposed = z_operator.T

    share = ny // cols
    planes = lax.all_to_all(scalar_field, "col", 0, 0, tiled=True)

    half = nx // rows // 2
    y_blocks = y_combined.reshape(rows, ny, rows, ny)
    by_distance = jnp.stack([y_blocks[me ^ d] for d in range(rows)])
    by_distance = jnp.stack([by_distance[:, :, me ^ d] for d in range(rows)], axis=2)
    by_distance = by_distance.reshape(rows * ny, rows, ny)

    def y_pencil(side):
        pieces = []
        for d in range(rows):
            first = (2 * (me ^ d) + side) * half
            piece = lax.dynamic_slice_in_dim(scalar_field, first, half, 2)
            pieces.append(piece if d == 0 else swap(piece, "row", rows, d))
        return jnp.concatenate(pieces, axis=0)

    def y_multiply(pencil):
        product = jnp.einsum(
            "yzx,ydk->dkzx", pencil, by_distance, preferred_element_type=jnp.float32
        ).astype(jnp.bfloat16)
        return [product[d] for d in range(rows)]

    def y_return(pieces):
        back = [pieces[d] if d == 0 else swap(pieces[d], "row", rows, d) for d in range(rows)]
        return [value.reshape(cols, share, nz, half) for value in back]

    pencils = [y_pencil(side) for side in range(2)]
    y_first_half, y_second_half = [y_multiply(pencil) for pencil in pencils]
    y_first_half = y_return(y_first_half)
    planes, y_first_half, y_second_half = lax.optimization_barrier(
        (planes, y_first_half, y_second_half)
    )
    y_second_half = y_return(y_second_half)

    planes = planes.reshape(cols, share, nz, nx)
    field = scalar_field.reshape(cols, share, nz, nx)
    where = me.reshape(1).astype(jnp.int32)
    sizes = chunk_sizes(share)
    starts = [sum(sizes[:c]) for c in range(len(sizes))]
    last = len(sizes) - 1

    def z_return(product):
        flat = product.reshape(-1, nz, nx)
        return lax.all_to_all(flat, "col", 0, 0, tiled=True).reshape(product.shape)

    def add_chunk(result, c):
        together = math.gcd(cols, 4 if c == last else 8)
        y_terms = y_first_half + y_second_half
        return total_into(
            result, starts[c], together, where, x_operator, field, z_back[c], y_terms
        )

    z_back, result = [], None
    for c in range(len(sizes)):
        product = z_apply(z_transposed, planes, starts[c], sizes[c])
        if c == last and last > 0:
            for earlier in range(last - 1):
                result = add_chunk(result, earlier)
            product, result = lax.optimization_barrier((product, result))
        elif c > 0:
            product, z_back[c - 1] = lax.optimization_barrier((product, z_back[c - 1]))
        z_back.append(z_return(product))
    for c in range(max(last - 1, 0), len(sizes)):
        result = add_chunk(result, c)
    return result.reshape(ny, nz, nx)


def solution(mesh):
    rows, cols = mesh.shape["row"], mesh.shape["col"]
    in_specs = (P("row", "col", None), P(), P(), P(), P(), P(), P())
    return jax.shard_map(
        functools.partial(per_device, rows, cols),
        mesh=mesh,
        in_specs=in_specs,
        out_specs=P("row", "col", None),
        check_vma=False,
    )
```

```python
import functools
import math

import jax
import jax.numpy as jnp
from jax import lax
from jax.experimental import pallas as pl
from jax.experimental.pallas import tpu as pltpu
from jax.sharding import PartitionSpec as P

VMEM_BYTES = 62 * 1024 * 1024


def z_kernel(operator_ref, field_ref, out_ref):
    parts, rows, depth, width = field_ref.shape
    for row in range(rows):
        planes = field_ref[:, row]
        if depth % 16:
            planes = planes.astype(jnp.float32)
        planes = planes.reshape(parts * depth, width).astype(jnp.bfloat16)
        product = jnp.dot(operator_ref[...], planes, preferred_element_type=jnp.float32)
        out_ref[:, row] = product.reshape(parts, depth, width).astype(jnp.bfloat16)


def z_apply(operator, field, first, count):
    parts, rows, depth, width = field.shape
    points = parts * depth
    step = math.gcd(math.gcd(first, count), 2)
    skip = first // step
    return pl.pallas_call(
        z_kernel,
        grid=(count // step,),
        in_specs=[
            pl.BlockSpec((points, points), lambda i: (0, 0)),
            pl.BlockSpec((parts, step, depth, width), lambda i: (0, i + skip, 0, 0)),
        ],
        out_specs=pl.BlockSpec((parts, step, depth, width), lambda i: (0, i, 0, 0)),
        out_shape=jax.ShapeDtypeStruct((parts, count, depth, width), jnp.bfloat16),
        compiler_params=pltpu.CompilerParams(vmem_limit_bytes=VMEM_BYTES),
        cost_estimate=pl.CostEstimate(
            flops=2 * points * points * count * width,
            bytes_accessed=4 * points * count * width,
            transcendentals=0,
        ),
    )(operator, field)


def z_pieces_kernel(operator_ref, field_ref, *out_refs):
    parts, _, depth, width = field_ref.shape
    planes = field_ref[:, 0]
    if depth % 16:
        planes = planes.astype(jnp.float32)
    planes = planes.reshape(parts * depth, width).astype(jnp.bfloat16)
    product = jnp.dot(operator_ref[...], planes, preferred_element_type=jnp.float32)
    for part, out_ref in enumerate(out_refs):
        out_ref[0] = product[part * depth : (part + 1) * depth].astype(jnp.bfloat16)


def z_pieces(operator, field, first, count):
    parts, _, depth, width = field.shape
    points = parts * depth
    return pl.pallas_call(
        z_pieces_kernel,
        grid=(count,),
        in_specs=[
            pl.BlockSpec((points, points), lambda i: (0, 0)),
            pl.BlockSpec((parts, 1, depth, width), lambda i: (0, i + first, 0, 0)),
        ],
        out_specs=[pl.BlockSpec((1, depth, width), lambda i: (i, 0, 0))] * parts,
        out_shape=[jax.ShapeDtypeStruct((count, depth, width), jnp.bfloat16)] * parts,
        compiler_params=pltpu.CompilerParams(vmem_limit_bytes=VMEM_BYTES),
        cost_estimate=pl.CostEstimate(
            flops=2 * points * points * count * width,
            bytes_accessed=4 * points * count * width,
            transcendentals=0,
        ),
    )(operator, field)


def total_kernel(slabs, pieces, place_ref, operator_ref, field_ref, *refs):
    if pieces > 1:
        z_ref = refs[-1]
        for distance in range(pieces):
            z_ref[place_ref[1] ^ distance] = refs[distance][...]
        out_ref = refs[-2]
    else:
        z_ref, out_ref = refs[0], refs[-1]
    y_refs = refs[pieces : pieces + 2 * slabs]
    parts, rows, depth, width = out_ref.shape
    slab = width // slabs
    share = slab // 2

    def add_all(me):
        flat = field_ref[...]
        if depth % 16:
            flat = flat.astype(jnp.float32)
        flat = flat.reshape(parts * rows * depth, width).astype(jnp.bfloat16)
        for owner in range(slabs):
            lanes = slice(owner * slab, (owner + 1) * slab)
            product = jnp.dot(flat, operator_ref[:, lanes], preferred_element_type=jnp.float32)
            product = product.reshape(parts, rows, depth, slab)
            for half in range(2):
                here = slice(owner * slab + half * share, owner * slab + (half + 1) * share)
                y_term = y_refs[half * slabs + (owner ^ me)][...].astype(jnp.float32)
                z_term = z_ref[:, :, :, here].astype(jnp.float32)
                x_term = product[:, :, :, half * share : (half + 1) * share]
                out_ref[:, :, :, here] = (x_term + y_term + z_term).astype(jnp.bfloat16)

    for me in range(slabs):
        pl.when(place_ref[0] == me)(functools.partial(add_all, me))


def total_into(so_far, first, together, place, operator, field, z_terms, y_terms):
    parts, _, depth, width = field.shape
    share = y_terms[0].shape[3]
    here = pl.BlockSpec((together, 1, depth, width), lambda p, i, r: (p, i + first, 0, 0))
    scratch = []
    if len(z_terms) == 1:
        count = z_terms[0].shape[1]
        z_spec = pl.BlockSpec((together, 1, depth, width), lambda p, i, r: (p, i, 0, 0))
    else:
        count, together = z_terms[0].shape[0], parts
        here = pl.BlockSpec((parts, 1, depth, width), lambda p, i, r: (p, i + first, 0, 0))
        z_spec = pl.BlockSpec((1, depth, width), lambda p, i, r: (i, 0, 0))
        scratch = [pltpu.VMEM((parts, 1, depth, width), jnp.bfloat16)]
    in_specs = [pl.BlockSpec((width, width), lambda p, i, r: (0, 0)), here]
    in_specs += [z_spec] * len(z_terms)
    in_specs += [
        pl.BlockSpec((together, 1, depth, share), lambda p, i, r: (p, i + first, 0, 0))
        for _ in y_terms
    ]
    operands = [operator, field, *z_terms, *y_terms]
    aliases = {}
    if so_far is not None:
        in_specs.append(pl.BlockSpec(memory_space=pl.ANY))
        operands.append(so_far)
        aliases = {len(operands): 0}
    return pl.pallas_call(
        functools.partial(total_kernel, len(y_terms) // 2, len(z_terms)),
        grid_spec=pltpu.PrefetchScalarGridSpec(
            num_scalar_prefetch=1,
            grid=(parts // together, count),
            in_specs=in_specs,
            out_specs=here,
            scratch_shapes=scratch,
        ),
        out_shape=jax.ShapeDtypeStruct(field.shape, jnp.bfloat16),
        input_output_aliases=aliases,
        compiler_params=pltpu.CompilerParams(vmem_limit_bytes=VMEM_BYTES),
        cost_estimate=pl.CostEstimate(
            flops=2 * width * width * parts * count * depth,
            bytes_accessed=8 * width * parts * count * depth,
            transcendentals=0,
        ),
    )(place, *operands)


def swap(value, axis, size, distance):
    return lax.ppermute(value, axis, [(i, i ^ distance) for i in range(size)])


def chunk_sizes(share):
    few = 2 if share >= 12 else 1
    return few, share - 2 * few, few


def per_device(rows, cols, scalar_field, x_operator, y_second, y_first, y_stretch, y_curve, z_operator):
    ny, nz, nx = scalar_field.shape
    me = lax.axis_index("row")
    y_combined = (
        y_stretch[None, :] * y_second.astype(jnp.float32)
        + y_curve[None, :] * y_first.astype(jnp.float32)
    ).astype(jnp.bfloat16)
    z_transposed = z_operator.T

    share = ny // cols
    planes = lax.all_to_all(scalar_field, "col", 0, 0, tiled=True)

    half = nx // rows // 2
    y_blocks = y_combined.reshape(rows, ny, rows, ny)
    by_distance = jnp.stack([y_blocks[me ^ d] for d in range(rows)])
    by_distance = jnp.stack([by_distance[:, :, me ^ d] for d in range(rows)], axis=2)
    by_distance = by_distance.reshape(rows * ny, rows, ny)

    def y_pencil(side):
        pieces = []
        for d in range(rows):
            first = (2 * (me ^ d) + side) * half
            piece = lax.dynamic_slice_in_dim(scalar_field, first, half, 2)
            pieces.append(piece if d == 0 else swap(piece, "row", rows, d))
        return jnp.concatenate(pieces, axis=0)

    def y_multiply(pencil):
        product = jnp.einsum(
            "yzx,ydk->dkzx", pencil, by_distance, preferred_element_type=jnp.float32
        ).astype(jnp.bfloat16)
        return [product[d] for d in range(rows)]

    def y_return(pieces):
        back = [pieces[d] if d == 0 else swap(pieces[d], "row", rows, d) for d in range(rows)]
        return [value.reshape(cols, share, nz, half) for value in back]

    pencils = [y_pencil(side) for side in range(2)]
    y_first_half, y_second_half = [y_multiply(pencil) for pencil in pencils]
    y_first_half = y_return(y_first_half)
    planes, y_first_half, y_second_half = lax.optimization_barrier(
        (planes, y_first_half, y_second_half)
    )
    y_terms = y_first_half + y_return(y_second_half)

    planes = planes.reshape(cols, share, nz, nx)
    field = scalar_field.reshape(cols, share, nz, nx)
    col = lax.axis_index("col")
    place = jnp.stack([me, col]).astype(jnp.int32)
    z_blocks = z_transposed.reshape(cols, nz, cols * nz)
    z_by_distance = jnp.concatenate([z_blocks[col ^ d] for d in range(cols)], axis=0)
    sizes = chunk_sizes(share)
    starts = [sum(sizes[:c]) for c in range(len(sizes))]

    def z_swap(pieces):
        return [pieces[d] if d == 0 else swap(pieces[d], "col", cols, d) for d in range(cols)]

    def z_return(product):
        flat = product.reshape(-1, nz, nx)
        return lax.all_to_all(flat, "col", 0, 0, tiled=True).reshape(product.shape)

    def add_chunk(result, c, together, z_terms):
        return total_into(
            result, starts[c], together, place, x_operator, field, z_terms, y_terms
        )

    far = cols // 2
    z_first = z_swap(z_pieces(z_by_distance, planes, starts[0], sizes[0]))
    bulk = z_apply(z_transposed, planes, starts[1], sizes[1])
    bulk, planes, z_first[far:] = lax.optimization_barrier((bulk, planes, z_first[far:]))
    z_bulk = z_return(bulk)

    product = z_apply(z_transposed, planes, starts[2], sizes[2])
    result = add_chunk(None, 0, cols, z_first)
    product, result = lax.optimization_barrier((product, result))
    z_last = z_return(product)

    result = add_chunk(result, 1, cols, [z_bulk])
    result = add_chunk(result, 2, math.gcd(cols, 4), [z_last])
    return result.reshape(ny, nz, nx)


def solution(mesh):
    rows, cols = mesh.shape["row"], mesh.shape["col"]
    in_specs = (P("row", "col", None), P(), P(), P(), P(), P(), P())
    return jax.shard_map(
        functools.partial(per_device, rows, cols),
        mesh=mesh,
        in_specs=in_specs,
        out_specs=P("row", "col", None),
        check_vma=False,
    )
```

```python
import functools
import math

import jax
import jax.numpy as jnp
from jax import lax
from jax.experimental import pallas as pl
from jax.experimental.pallas import tpu as pltpu
from jax.sharding import PartitionSpec as P

VMEM_BYTES = 62 * 1024 * 1024


def z_kernel(operator_ref, field_ref, out_ref):
    parts, rows, depth, width = field_ref.shape
    for row in range(rows):
        planes = field_ref[:, row]
        if depth % 16:
            planes = planes.astype(jnp.float32)
        planes = planes.reshape(parts * depth, width).astype(jnp.bfloat16)
        product = jnp.dot(operator_ref[...], planes, preferred_element_type=jnp.float32)
        out_ref[:, row] = product.reshape(parts, depth, width).astype(jnp.bfloat16)


def z_apply(operator, field, first, count):
    parts, rows, depth, width = field.shape
    points = parts * depth
    step = math.gcd(math.gcd(first, count), 2)
    skip = first // step
    return pl.pallas_call(
        z_kernel,
        grid=(count // step,),
        in_specs=[
            pl.BlockSpec((points, points), lambda i: (0, 0)),
            pl.BlockSpec((parts, step, depth, width), lambda i: (0, i + skip, 0, 0)),
        ],
        out_specs=pl.BlockSpec((parts, step, depth, width), lambda i: (0, i, 0, 0)),
        out_shape=jax.ShapeDtypeStruct((parts, count, depth, width), jnp.bfloat16),
        compiler_params=pltpu.CompilerParams(vmem_limit_bytes=VMEM_BYTES),
        cost_estimate=pl.CostEstimate(
            flops=2 * points * points * count * width,
            bytes_accessed=4 * points * count * width,
            transcendentals=0,
        ),
    )(operator, field)


def z_pieces_kernel(operator_ref, field_ref, *out_refs):
    parts, _, depth, width = field_ref.shape
    planes = field_ref[:, 0]
    if depth % 16:
        planes = planes.astype(jnp.float32)
    planes = planes.reshape(parts * depth, width).astype(jnp.bfloat16)
    product = jnp.dot(operator_ref[...], planes, preferred_element_type=jnp.float32)
    for part, out_ref in enumerate(out_refs):
        out_ref[0] = product[part * depth : (part + 1) * depth].astype(jnp.bfloat16)


def z_pieces(operator, field, first, count):
    parts, _, depth, width = field.shape
    points = parts * depth
    return pl.pallas_call(
        z_pieces_kernel,
        grid=(count,),
        in_specs=[
            pl.BlockSpec((points, points), lambda i: (0, 0)),
            pl.BlockSpec((parts, 1, depth, width), lambda i: (0, i + first, 0, 0)),
        ],
        out_specs=[pl.BlockSpec((1, depth, width), lambda i: (i, 0, 0))] * parts,
        out_shape=[jax.ShapeDtypeStruct((count, depth, width), jnp.bfloat16)] * parts,
        compiler_params=pltpu.CompilerParams(vmem_limit_bytes=VMEM_BYTES),
        cost_estimate=pl.CostEstimate(
            flops=2 * points * points * count * width,
            bytes_accessed=4 * points * count * width,
            transcendentals=0,
        ),
    )(operator, field)


def total_kernel(slabs, pieces, place_ref, operator_ref, field_ref, *refs):
    if pieces > 1:
        z_ref = refs[-1]
        for distance in range(pieces):
            z_ref[place_ref[1] ^ distance] = refs[distance][...]
        out_ref = refs[-2]
    else:
        z_ref, out_ref = refs[0], refs[-1]
    y_refs = refs[pieces : pieces + 2 * slabs]
    parts, rows, depth, width = out_ref.shape
    slab = width // slabs
    share = slab // 2

    def add_all(me):
        flat = field_ref[...]
        if depth % 16:
            flat = flat.astype(jnp.float32)
        flat = flat.reshape(parts * rows * depth, width).astype(jnp.bfloat16)
        for owner in range(slabs):
            lanes = slice(owner * slab, (owner + 1) * slab)
            product = jnp.dot(flat, operator_ref[:, lanes], preferred_element_type=jnp.float32)
            product = product.reshape(parts, rows, depth, slab)
            for half in range(2):
                here = slice(owner * slab + half * share, owner * slab + (half + 1) * share)
                y_term = y_refs[half * slabs + (owner ^ me)][...].astype(jnp.float32)
                z_term = z_ref[:, :, :, here].astype(jnp.float32)
                x_term = product[:, :, :, half * share : (half + 1) * share]
                out_ref[:, :, :, here] = (x_term + y_term + z_term).astype(jnp.bfloat16)

    for me in range(slabs):
        pl.when(place_ref[0] == me)(functools.partial(add_all, me))


def total_into(so_far, first, together, place, operator, field, z_terms, y_terms):
    parts, _, depth, width = field.shape
    share = y_terms[0].shape[3]
    here = pl.BlockSpec((together, 1, depth, width), lambda p, i, r: (p, i + first, 0, 0))
    scratch = []
    if len(z_terms) == 1:
        count = z_terms[0].shape[1]
        z_spec = pl.BlockSpec((together, 1, depth, width), lambda p, i, r: (p, i, 0, 0))
    else:
        count, together = z_terms[0].shape[0], parts
        here = pl.BlockSpec((parts, 1, depth, width), lambda p, i, r: (p, i + first, 0, 0))
        z_spec = pl.BlockSpec((1, depth, width), lambda p, i, r: (i, 0, 0))
        scratch = [pltpu.VMEM((parts, 1, depth, width), jnp.bfloat16)]
    in_specs = [pl.BlockSpec((width, width), lambda p, i, r: (0, 0)), here]
    in_specs += [z_spec] * len(z_terms)
    in_specs += [
        pl.BlockSpec((together, 1, depth, share), lambda p, i, r: (p, i + first, 0, 0))
        for _ in y_terms
    ]
    operands = [operator, field, *z_terms, *y_terms]
    aliases = {}
    if so_far is not None:
        in_specs.append(pl.BlockSpec(memory_space=pl.ANY))
        operands.append(so_far)
        aliases = {len(operands): 0}
    return pl.pallas_call(
        functools.partial(total_kernel, len(y_terms) // 2, len(z_terms)),
        grid_spec=pltpu.PrefetchScalarGridSpec(
            num_scalar_prefetch=1,
            grid=(parts // together, count),
            in_specs=in_specs,
            out_specs=here,
            scratch_shapes=scratch,
        ),
        out_shape=jax.ShapeDtypeStruct(field.shape, jnp.bfloat16),
        input_output_aliases=aliases,
        compiler_params=pltpu.CompilerParams(vmem_limit_bytes=VMEM_BYTES),
        cost_estimate=pl.CostEstimate(
            flops=2 * width * width * parts * count * depth,
            bytes_accessed=8 * width * parts * count * depth,
            transcendentals=0,
        ),
    )(place, *operands)


def base_kernel(slabs, place_ref, operator_ref, field_ref, *refs):
    y_refs, out_ref = refs[:-1], refs[-1]
    parts, rows, depth, width = out_ref.shape
    slab = width // slabs
    share = slab // 2

    def add_all(me):
        flat = field_ref[...]
        if depth % 16:
            flat = flat.astype(jnp.float32)
        flat = flat.reshape(parts * rows * depth, width).astype(jnp.bfloat16)
        for owner in range(slabs):
            lanes = slice(owner * slab, (owner + 1) * slab)
            product = jnp.dot(flat, operator_ref[:, lanes], preferred_element_type=jnp.float32)
            product = product.reshape(parts, rows, depth, slab)
            for half in range(2):
                here = slice(owner * slab + half * share, owner * slab + (half + 1) * share)
                y_term = y_refs[half * slabs + (owner ^ me)][...].astype(jnp.float32)
                x_term = product[:, :, :, half * share : (half + 1) * share]
                out_ref[:, :, :, here] = x_term + y_term

    for me in range(slabs):
        pl.when(place_ref[0] == me)(functools.partial(add_all, me))


def x_and_y(first, count, together, place, operator, field, y_terms):
    parts, _, depth, width = field.shape
    share = y_terms[0].shape[3]
    where = lambda p, i, r: (p, i + first, 0, 0)
    return pl.pallas_call(
        functools.partial(base_kernel, len(y_terms) // 2),
        grid_spec=pltpu.PrefetchScalarGridSpec(
            num_scalar_prefetch=1,
            grid=(parts // together, count),
            in_specs=[
                pl.BlockSpec((width, width), lambda p, i, r: (0, 0)),
                pl.BlockSpec((together, 1, depth, width), where),
            ]
            + [pl.BlockSpec((together, 1, depth, share), where) for _ in y_terms],
            out_specs=pl.BlockSpec((together, 1, depth, width), lambda p, i, r: (p, i, 0, 0)),
        ),
        out_shape=jax.ShapeDtypeStruct((parts, count, depth, width), jnp.float32),
        compiler_params=pltpu.CompilerParams(vmem_limit_bytes=VMEM_BYTES),
        cost_estimate=pl.CostEstimate(
            flops=2 * width * width * parts * count * depth,
            bytes_accessed=8 * width * parts * count * depth,
            transcendentals=0,
        ),
    )(place, operator, field, *y_terms)


def add_kernel(base_ref, z_ref, so_far_ref, out_ref):
    out_ref[...] = (base_ref[...] + z_ref[...].astype(jnp.float32)).astype(jnp.bfloat16)


def add_into(so_far, first, base, z_term):
    parts, count, depth, width = z_term.shape
    step = math.gcd(first, count)
    skip = first // step
    block = pl.BlockSpec((1, step, depth, width), lambda p, i: (p, i, 0, 0))
    return pl.pallas_call(
        add_kernel,
        grid=(parts, count // step),
        in_specs=[block, block, pl.BlockSpec(memory_space=pl.ANY)],
        out_specs=pl.BlockSpec((1, step, depth, width), lambda p, i: (p, i + skip, 0, 0)),
        out_shape=jax.ShapeDtypeStruct(so_far.shape, jnp.bfloat16),
        input_output_aliases={2: 0},
        compiler_params=pltpu.CompilerParams(vmem_limit_bytes=VMEM_BYTES),
        cost_estimate=pl.CostEstimate(
            flops=width * parts * count * depth,
            bytes_accessed=8 * width * parts * count * depth,
            transcendentals=0,
        ),
    )(base, z_term, so_far)


def swap(value, axis, size, distance):
    return lax.ppermute(value, axis, [(i, i ^ distance) for i in range(size)])


def chunk_sizes(share):
    few = 2 if share >= 12 else 1
    return few, share - 2 * few, few


def per_device(rows, cols, scalar_field, x_operator, y_second, y_first, y_stretch, y_curve, z_operator):
    ny, nz, nx = scalar_field.shape
    me = lax.axis_index("row")
    y_combined = (
        y_stretch[None, :] * y_second.astype(jnp.float32)
        + y_curve[None, :] * y_first.astype(jnp.float32)
    ).astype(jnp.bfloat16)
    z_transposed = z_operator.T

    share = ny // cols
    planes = lax.all_to_all(scalar_field, "col", 0, 0, tiled=True)

    half = nx // rows // 2
    y_blocks = y_combined.reshape(rows, ny, rows, ny)
    by_distance = jnp.stack([y_blocks[me ^ d] for d in range(rows)])
    by_distance = jnp.stack([by_distance[:, :, me ^ d] for d in range(rows)], axis=2)
    by_distance = by_distance.reshape(rows * ny, rows, ny)

    def y_pencil(side):
        pieces = []
        for d in range(rows):
            first = (2 * (me ^ d) + side) * half
            piece = lax.dynamic_slice_in_dim(scalar_field, first, half, 2)
            pieces.append(piece if d == 0 else swap(piece, "row", rows, d))
        return jnp.concatenate(pieces, axis=0)

    def y_multiply(pencil):
        product = jnp.einsum(
            "yzx,ydk->dkzx", pencil, by_distance, preferred_element_type=jnp.float32
        ).astype(jnp.bfloat16)
        return [product[d] for d in range(rows)]

    def y_return(pieces):
        back = [pieces[d] if d == 0 else swap(pieces[d], "row", rows, d) for d in range(rows)]
        return [value.reshape(cols, share, nz, half) for value in back]

    pencils = [y_pencil(side) for side in range(2)]
    y_first_half, y_second_half = [y_multiply(pencil) for pencil in pencils]
    y_first_half = y_return(y_first_half)
    planes, y_first_half, y_second_half = lax.optimization_barrier(
        (planes, y_first_half, y_second_half)
    )
    y_terms = y_first_half + y_return(y_second_half)

    planes = planes.reshape(cols, share, nz, nx)
    field = scalar_field.reshape(cols, share, nz, nx)
    col = lax.axis_index("col")
    place = jnp.stack([me, col]).astype(jnp.int32)
    z_blocks = z_transposed.reshape(cols, nz, cols * nz)
    z_by_distance = jnp.concatenate([z_blocks[col ^ d] for d in range(cols)], axis=0)
    sizes = chunk_sizes(share)
    starts = [sum(sizes[:c]) for c in range(len(sizes))]

    def z_swap(pieces):
        return [pieces[d] if d == 0 else swap(pieces[d], "col", cols, d) for d in range(cols)]

    def z_return(product):
        flat = product.reshape(-1, nz, nx)
        return lax.all_to_all(flat, "col", 0, 0, tiled=True).reshape(product.shape)

    def add_chunk(result, c, together, z_terms):
        return total_into(
            result, starts[c], together, place, x_operator, field, z_terms, y_terms
        )

    far = cols // 2
    z_first = z_swap(z_pieces(z_by_distance, planes, starts[0], sizes[0]))
    bulk = z_apply(z_transposed, planes, starts[1], sizes[1])
    bulk, planes, z_first[far:] = lax.optimization_barrier((bulk, planes, z_first[far:]))
    z_bulk = z_return(bulk)

    product = z_apply(z_transposed, planes, starts[2], sizes[2])
    result = add_chunk(None, 0, cols, z_first)
    base = x_and_y(starts[2], sizes[2], cols, place, x_operator, field, y_terms)
    product, result, base = lax.optimization_barrier((product, result, base))
    z_last = z_return(product)

    result = add_chunk(result, 1, cols, [z_bulk])
    result = add_into(result, starts[2], base, z_last)
    return result.reshape(ny, nz, nx)


def solution(mesh):
    rows, cols = mesh.shape["row"], mesh.shape["col"]
    in_specs = (P("row", "col", None), P(), P(), P(), P(), P(), P())
    return jax.shard_map(
        functools.partial(per_device, rows, cols),
        mesh=mesh,
        in_specs=in_specs,
        out_specs=P("row", "col", None),
        check_vma=False,
    )
```

```python
import functools
import math

import jax
import jax.numpy as jnp
from jax import lax
from jax.experimental import pallas as pl
from jax.experimental.pallas import tpu as pltpu
from jax.sharding import PartitionSpec as P

VMEM_BYTES = 62 * 1024 * 1024


def z_kernel(operator_ref, field_ref, out_ref):
    parts, rows, depth, width = field_ref.shape
    for row in range(rows):
        planes = field_ref[:, row]
        if depth % 16:
            planes = planes.astype(jnp.float32)
        planes = planes.reshape(parts * depth, width).astype(jnp.bfloat16)
        product = jnp.dot(operator_ref[...], planes, preferred_element_type=jnp.float32)
        out_ref[:, row] = product.reshape(parts, depth, width).astype(jnp.bfloat16)


def z_apply(operator, field, first, count):
    parts, rows, depth, width = field.shape
    points = parts * depth
    step = math.gcd(math.gcd(first, count), 2)
    skip = first // step
    return pl.pallas_call(
        z_kernel,
        grid=(count // step,),
        in_specs=[
            pl.BlockSpec((points, points), lambda i: (0, 0)),
            pl.BlockSpec((parts, step, depth, width), lambda i: (0, i + skip, 0, 0)),
        ],
        out_specs=pl.BlockSpec((parts, step, depth, width), lambda i: (0, i, 0, 0)),
        out_shape=jax.ShapeDtypeStruct((parts, count, depth, width), jnp.bfloat16),
        compiler_params=pltpu.CompilerParams(vmem_limit_bytes=VMEM_BYTES),
        cost_estimate=pl.CostEstimate(
            flops=2 * points * points * count * width,
            bytes_accessed=4 * points * count * width,
            transcendentals=0,
        ),
    )(operator, field)


def z_pieces_kernel(operator_ref, field_ref, *out_refs):
    parts, _, depth, width = field_ref.shape
    planes = field_ref[:, 0]
    if depth % 16:
        planes = planes.astype(jnp.float32)
    planes = planes.reshape(parts * depth, width).astype(jnp.bfloat16)
    product = jnp.dot(operator_ref[...], planes, preferred_element_type=jnp.float32)
    for part, out_ref in enumerate(out_refs):
        out_ref[0] = product[part * depth : (part + 1) * depth].astype(jnp.bfloat16)


def z_pieces(operator, field, first, count):
    parts, _, depth, width = field.shape
    points = parts * depth
    return pl.pallas_call(
        z_pieces_kernel,
        grid=(count,),
        in_specs=[
            pl.BlockSpec((points, points), lambda i: (0, 0)),
            pl.BlockSpec((parts, 1, depth, width), lambda i: (0, i + first, 0, 0)),
        ],
        out_specs=[pl.BlockSpec((1, depth, width), lambda i: (i, 0, 0))] * parts,
        out_shape=[jax.ShapeDtypeStruct((count, depth, width), jnp.bfloat16)] * parts,
        compiler_params=pltpu.CompilerParams(vmem_limit_bytes=VMEM_BYTES),
        cost_estimate=pl.CostEstimate(
            flops=2 * points * points * count * width,
            bytes_accessed=4 * points * count * width,
            transcendentals=0,
        ),
    )(operator, field)


def total_kernel(slabs, pieces, place_ref, operator_ref, field_ref, *refs):
    if pieces > 1:
        z_ref = refs[-1]
        for distance in range(pieces):
            z_ref[place_ref[1] ^ distance] = refs[distance][...]
        out_ref = refs[-2]
    else:
        z_ref, out_ref = refs[0], refs[-1]
    y_refs = refs[pieces : pieces + 2 * slabs]
    parts, rows, depth, width = out_ref.shape
    slab = width // slabs
    share = slab // 2

    def add_all(me):
        flat = field_ref[...]
        if depth % 16:
            flat = flat.astype(jnp.float32)
        flat = flat.reshape(parts * rows * depth, width).astype(jnp.bfloat16)
        for owner in range(slabs):
            lanes = slice(owner * slab, (owner + 1) * slab)
            product = jnp.dot(flat, operator_ref[:, lanes], preferred_element_type=jnp.float32)
            product = product.reshape(parts, rows, depth, slab)
            for half in range(2):
                here = slice(owner * slab + half * share, owner * slab + (half + 1) * share)
                y_term = y_refs[half * slabs + (owner ^ me)][...].astype(jnp.float32)
                z_term = z_ref[:, :, :, here].astype(jnp.float32)
                x_term = product[:, :, :, half * share : (half + 1) * share]
                out_ref[:, :, :, here] = (x_term + y_term + z_term).astype(jnp.bfloat16)

    for me in range(slabs):
        pl.when(place_ref[0] == me)(functools.partial(add_all, me))


def total_into(so_far, first, together, place, operator, field, z_terms, y_terms):
    parts, _, depth, width = field.shape
    share = y_terms[0].shape[3]
    here = pl.BlockSpec((together, 1, depth, width), lambda p, i, r: (p, i + first, 0, 0))
    scratch = []
    if len(z_terms) == 1:
        count = z_terms[0].shape[1]
        z_spec = pl.BlockSpec((together, 1, depth, width), lambda p, i, r: (p, i, 0, 0))
    else:
        count, together = z_terms[0].shape[0], parts
        here = pl.BlockSpec((parts, 1, depth, width), lambda p, i, r: (p, i + first, 0, 0))
        z_spec = pl.BlockSpec((1, depth, width), lambda p, i, r: (i, 0, 0))
        scratch = [pltpu.VMEM((parts, 1, depth, width), jnp.bfloat16)]
    in_specs = [pl.BlockSpec((width, width), lambda p, i, r: (0, 0)), here]
    in_specs += [z_spec] * len(z_terms)
    in_specs += [
        pl.BlockSpec((together, 1, depth, share), lambda p, i, r: (p, i + first, 0, 0))
        for _ in y_terms
    ]
    operands = [operator, field, *z_terms, *y_terms]
    aliases = {}
    if so_far is not None:
        in_specs.append(pl.BlockSpec(memory_space=pl.ANY))
        operands.append(so_far)
        aliases = {len(operands): 0}
    return pl.pallas_call(
        functools.partial(total_kernel, len(y_terms) // 2, len(z_terms)),
        grid_spec=pltpu.PrefetchScalarGridSpec(
            num_scalar_prefetch=1,
            grid=(parts // together, count),
            in_specs=in_specs,
            out_specs=here,
            scratch_shapes=scratch,
        ),
        out_shape=jax.ShapeDtypeStruct(field.shape, jnp.bfloat16),
        input_output_aliases=aliases,
        compiler_params=pltpu.CompilerParams(vmem_limit_bytes=VMEM_BYTES),
        cost_estimate=pl.CostEstimate(
            flops=2 * width * width * parts * count * depth,
            bytes_accessed=8 * width * parts * count * depth,
            transcendentals=0,
        ),
    )(place, *operands)


def base_kernel(slabs, place_ref, operator_ref, field_ref, *refs):
    y_refs, out_ref = refs[:-1], refs[-1]
    parts, rows, depth, width = out_ref.shape
    slab = width // slabs
    share = slab // 2

    def add_all(me):
        flat = field_ref[...]
        if depth % 16:
            flat = flat.astype(jnp.float32)
        flat = flat.reshape(parts * rows * depth, width).astype(jnp.bfloat16)
        for owner in range(slabs):
            lanes = slice(owner * slab, (owner + 1) * slab)
            product = jnp.dot(flat, operator_ref[:, lanes], preferred_element_type=jnp.float32)
            product = product.reshape(parts, rows, depth, slab)
            for half in range(2):
                here = slice(owner * slab + half * share, owner * slab + (half + 1) * share)
                y_term = y_refs[half * slabs + (owner ^ me)][...].astype(jnp.float32)
                x_term = product[:, :, :, half * share : (half + 1) * share]
                out_ref[:, :, :, here] = x_term + y_term

    for me in range(slabs):
        pl.when(place_ref[0] == me)(functools.partial(add_all, me))


def x_and_y(first, count, together, place, operator, field, y_terms):
    parts, _, depth, width = field.shape
    share = y_terms[0].shape[3]
    where = lambda p, i, r: (p, i + first, 0, 0)
    return pl.pallas_call(
        functools.partial(base_kernel, len(y_terms) // 2),
        grid_spec=pltpu.PrefetchScalarGridSpec(
            num_scalar_prefetch=1,
            grid=(parts // together, count),
            in_specs=[
                pl.BlockSpec((width, width), lambda p, i, r: (0, 0)),
                pl.BlockSpec((together, 1, depth, width), where),
            ]
            + [pl.BlockSpec((together, 1, depth, share), where) for _ in y_terms],
            out_specs=pl.BlockSpec((together, 1, depth, width), lambda p, i, r: (p, i, 0, 0)),
        ),
        out_shape=jax.ShapeDtypeStruct((parts, count, depth, width), jnp.float32),
        compiler_params=pltpu.CompilerParams(vmem_limit_bytes=VMEM_BYTES),
        cost_estimate=pl.CostEstimate(
            flops=2 * width * width * parts * count * depth,
            bytes_accessed=8 * width * parts * count * depth,
            transcendentals=0,
        ),
    )(place, operator, field, *y_terms)


def add_kernel(base_ref, z_ref, so_far_ref, out_ref):
    out_ref[...] = (base_ref[...] + z_ref[...].astype(jnp.float32)).astype(jnp.bfloat16)


def add_into(so_far, first, base, z_term):
    parts, count, depth, width = z_term.shape
    step = math.gcd(first, count)
    skip = first // step
    together = math.gcd(parts, 4)
    block = pl.BlockSpec((together, step, depth, width), lambda p, i: (p, i, 0, 0))
    return pl.pallas_call(
        add_kernel,
        grid=(parts // together, count // step),
        in_specs=[block, block, pl.BlockSpec(memory_space=pl.ANY)],
        out_specs=pl.BlockSpec((together, step, depth, width), lambda p, i: (p, i + skip, 0, 0)),
        out_shape=jax.ShapeDtypeStruct(so_far.shape, jnp.bfloat16),
        input_output_aliases={2: 0},
        compiler_params=pltpu.CompilerParams(vmem_limit_bytes=VMEM_BYTES),
        cost_estimate=pl.CostEstimate(
            flops=width * parts * count * depth,
            bytes_accessed=8 * width * parts * count * depth,
            transcendentals=0,
        ),
    )(base, z_term, so_far)


def swap(value, axis, size, distance):
    return lax.ppermute(value, axis, [(i, i ^ distance) for i in range(size)])


def chunk_sizes(share):
    few = 2 if share >= 12 else 1
    return few, share - 2 * few, few


def per_device(rows, cols, scalar_field, x_operator, y_second, y_first, y_stretch, y_curve, z_operator):
    ny, nz, nx = scalar_field.shape
    me = lax.axis_index("row")
    y_combined = (
        y_stretch[None, :] * y_second.astype(jnp.float32)
        + y_curve[None, :] * y_first.astype(jnp.float32)
    ).astype(jnp.bfloat16)
    z_transposed = z_operator.T

    share = ny // cols
    planes = lax.all_to_all(scalar_field, "col", 0, 0, tiled=True)

    half = nx // rows // 2
    y_blocks = y_combined.reshape(rows, ny, rows, ny)
    by_distance = jnp.stack([y_blocks[me ^ d] for d in range(rows)])
    by_distance = jnp.stack([by_distance[:, :, me ^ d] for d in range(rows)], axis=2)
    by_distance = by_distance.reshape(rows * ny, rows, ny)

    def y_pencil(side):
        pieces = []
        for d in range(rows):
            first = (2 * (me ^ d) + side) * half
            piece = lax.dynamic_slice_in_dim(scalar_field, first, half, 2)
            pieces.append(piece if d == 0 else swap(piece, "row", rows, d))
        return jnp.concatenate(pieces, axis=0)

    def y_multiply(pencil):
        product = jnp.einsum(
            "yzx,ydk->dkzx", pencil, by_distance, preferred_element_type=jnp.float32
        ).astype(jnp.bfloat16)
        return [product[d] for d in range(rows)]

    def y_return(pieces):
        back = [pieces[d] if d == 0 else swap(pieces[d], "row", rows, d) for d in range(rows)]
        return [value.reshape(cols, share, nz, half) for value in back]

    pencils = [y_pencil(side) for side in range(2)]
    y_first_half, y_second_half = [y_multiply(pencil) for pencil in pencils]
    y_first_half = y_return(y_first_half)
    planes, y_first_half, y_second_half = lax.optimization_barrier(
        (planes, y_first_half, y_second_half)
    )
    y_terms = y_first_half + y_return(y_second_half)

    planes = planes.reshape(cols, share, nz, nx)
    field = scalar_field.reshape(cols, share, nz, nx)
    col = lax.axis_index("col")
    place = jnp.stack([me, col]).astype(jnp.int32)
    z_blocks = z_transposed.reshape(cols, nz, cols * nz)
    z_by_distance = jnp.concatenate([z_blocks[col ^ d] for d in range(cols)], axis=0)
    sizes = chunk_sizes(share)
    starts = [sum(sizes[:c]) for c in range(len(sizes))]

    def z_swap(pieces):
        return [pieces[d] if d == 0 else swap(pieces[d], "col", cols, d) for d in range(cols)]

    def z_return(product):
        flat = product.reshape(-1, nz, nx)
        return lax.all_to_all(flat, "col", 0, 0, tiled=True).reshape(product.shape)

    def add_chunk(result, c, together, z_terms):
        return total_into(
            result, starts[c], together, place, x_operator, field, z_terms, y_terms
        )

    far = cols // 2
    z_first = z_swap(z_pieces(z_by_distance, planes, starts[0], sizes[0]))
    bulk = z_apply(z_transposed, planes, starts[1], sizes[1])
    bulk, planes, z_first[far:] = lax.optimization_barrier((bulk, planes, z_first[far:]))
    z_bulk = z_return(bulk)

    product = z_apply(z_transposed, planes, starts[2], sizes[2])
    result = add_chunk(None, 0, cols, z_first)
    base = x_and_y(starts[2], sizes[2], cols, place, x_operator, field, y_terms)
    product, result, base = lax.optimization_barrier((product, result, base))
    z_last = z_return(product)

    result = add_chunk(result, 1, cols, [z_bulk])
    result = add_into(result, starts[2], base, z_last)
    return result.reshape(ny, nz, nx)


def solution(mesh):
    rows, cols = mesh.shape["row"], mesh.shape["col"]
    in_specs = (P("row", "col", None), P(), P(), P(), P(), P(), P())
    return jax.shard_map(
        functools.partial(per_device, rows, cols),
        mesh=mesh,
        in_specs=in_specs,
        out_specs=P("row", "col", None),
        check_vma=False,
    )
```
